32 devices in a mesh: beams: 2 (over y), tm: 4 (over x, core), band: 4 (over z).
Axes of the slice: x: 2, y: 2, z: 4, core: 2. Of those that a mesh axis runs over, the one named last changes fastest.
Arguments:
- signal: float32 [512, 131072], P(('beams', 'band'), 'tm'), parts along dimension 0, may hold values from -6 to 6
- tree_picks: int32 [2, 8, 256], replicated, may hold values from 0 to 63, as said below
- tree_delays: int32 [8, 256], replicated, may hold values from 0 to 4
- template_bank: float32 [2, 201, 64], replicated, may hold values from -0.75 to 0.75
- template_pick: int32 [8, 64, 2], P(('beams', 'band'), 'tm'), parts along dimension 0, may hold values from 0 to 200
Outputs:
- powers: float32 [8, 64, 2, 65536], P(('beams', 'band'), 'tm'), parts along dimension 0
The draws below stay inside these ranges and needn't reach their ends.
There are 2 independent parts, one for each index of `beams`. The reference program is written for one: setup_inputs(seed, part) draws one part's arguments, and reference() takes and returns one part's arrays. A program takes and returns all parts, laid end to end along the dimension named above; an argument that names none is the same for every part. Nothing has to cross between parts.
Inputs may be any that keep to these rules, and one draw needn't show every extreme that they name: `tree_picks`: entries of section j are below the smaller of 2 to the power j and 64.
All inputs are finite; a program needn't handle non-finite values.
Results may differ from the reference program's by a relative error of at most 0.00007.
Values sent between devices are 32-bit elements; how exact they have to be, the bound alone decides.
A program may use at most 192 MiB of HBM per device.

```python
import math
import jax
import jax.numpy as jnp
from jax import lax

CH_DEV = 64
SAMPLES = 131072
MAXD = 4
TAPS = 64
ZBANK = 201
ZSEL = 2
SUBBANDS = 4
CHANNELS = 256
SECTIONS = 8
FREQS = 65536


def draw_tree_picks(key, part):
    sub_key = jax.random.fold_in(key, 11)
    section_iota = jnp.arange(SECTIONS, dtype=jnp.int32)
    upper_bound = jnp.minimum(jnp.left_shift(jnp.int32(1), section_iota), CH_DEV)
    picks = jax.random.randint(sub_key, (2, SECTIONS, CHANNELS), 0, upper_bound[None, :, None], dtype=jnp.int32)
    return picks.at[:, SECTIONS - 1, 0].set(CH_DEV - 1)


def draw_tree_delays(key, part):
    sub_key = jax.random.fold_in(key, 23)
    delays = jax.random.randint(sub_key, (SECTIONS, CHANNELS), 0, MAXD + 1, dtype=jnp.int32)
    return delays.at[:, 0].set(MAXD)


def with_ends(values, stream_key, smallest, high):
    dims = values.shape
    place = [jax.random.randint(jax.random.fold_in(stream_key, axis), (), 0, dims[axis]) for axis in range(len(dims))]
    values = values.at[tuple(place)].set(smallest)
    longest = dims.index(max(dims))
    place[longest] = (place[longest] + 1) % dims[longest]
    return values.at[tuple(place)].set(high)


def block_scale(rng, dims, pieces, smallest, high):
    level = 1.0
    for position, shards_of in pieces:
        draws = jax.random.uniform(jax.random.fold_in(jax.random.fold_in(rng, 6), position), (shards_of,), jnp.float32, smallest / len(pieces), high / len(pieces))
        level = level * jnp.repeat(jnp.exp(draws), dims[position] // shards_of).reshape((-1,) + (1,) * (len(dims) - 1 - position))
    return level


def scatter_about(rng, extent, width, reach, split=(), kind=jnp.bfloat16):
    factor_of = block_scale(rng, extent, split, -0.22, 0.18) if split else 1.0
    result = jax.random.normal(rng, extent, jnp.float32) * width * factor_of
    return jnp.minimum(jnp.maximum(result, -reach), reach).astype(kind)


def setup_inputs(seed: int = 0, part: int = 0) -> dict:
    key_list = jax.random.split(jax.random.key(seed), 6)
    own_keys = jax.random.split(jax.random.fold_in(key_list[5], part), 6)
    return {
        "signal": scatter_about(own_keys[0], (CHANNELS, SAMPLES), 1.0, 6.0, ((0, 4), (1, 4)), jnp.float32),
        "tree_picks": draw_tree_picks(jax.random.fold_in(key_list[5], 71), part),
        "tree_delays": draw_tree_delays(jax.random.fold_in(key_list[5], 71), part),
        "template_bank": scatter_about(key_list[3], (2, ZBANK, TAPS), 0.125, 0.75, (), jnp.float32),
        "template_pick": with_ends(jax.random.randint(own_keys[4], (SUBBANDS, CH_DEV, ZSEL), 0, ZBANK), jax.random.fold_in(own_keys[4], 1), 0, ZBANK - 1).astype(jnp.int32),
    }


def delayed_rows(upper_rows, delays, out_len):
    total = jnp.zeros((upper_rows.shape[0], out_len), upper_rows.dtype)
    for shift_by in range(MAXD + 1):
        total = total + jnp.where(delays[:, None] == shift_by, upper_rows[:, shift_by:shift_by + out_len], 0.0)
    return total

def group_section(block, section_num, first_row, pick_low, pick_high, delays, out_len):
    row_count = block.shape[0]
    half_size = 1 << section_num
    global_row = first_row + jnp.arange(row_count, dtype=jnp.int32)
    base_row = global_row - global_row % (2 * half_size) + global_row % half_size - global_row % min(half_size, CH_DEV) - first_row
    low_rows = jnp.take(block, (base_row + pick_low).astype(jnp.int32), axis=0)
    high_rows = jnp.take(block, (base_row + half_size + pick_high).astype(jnp.int32), axis=0)
    return low_rows[:, :out_len] + delayed_rows(high_rows, delays.astype(jnp.int32), out_len)

def template_powers(spec_re, spec_im, tmpl_re, tmpl_im):
    trials, freq_count = spec_re.shape
    tap_count = tmpl_re.shape[-1]
    block_count = freq_count // 128
    highest = lax.Precision.HIGHEST

    def windows(spectrum):
        padded = jnp.pad(spectrum, ((0, 0), (tap_count // 2, 128 - tap_count // 2)))
        tiles = padded.reshape(trials, block_count + 1, 128)
        return jnp.concatenate([tiles[:, :-1], tiles[:, 1:, :tap_count]], axis=2)
    lag_matrix = jnp.arange(128 + tap_count, dtype=jnp.int32)[:, None] - jnp.arange(128, dtype=jnp.int32)[None, :]
    in_band = (lag_matrix >= 0) & (lag_matrix < tap_count)
    lag_index = jnp.clip(lag_matrix, 0, tap_count - 1)
    band_re = jnp.where(in_band, tmpl_re[..., lag_index], 0.0)
    band_im = jnp.where(in_band, tmpl_im[..., lag_index], 0.0)
    win_re = windows(spec_re)
    win_im = windows(spec_im)
    out_re = jnp.einsum('tbj,tzji->tzbi', win_re, band_re, precision=highest) - jnp.einsum('tbj,tzji->tzbi', win_im, band_im, precision=highest)
    out_im = jnp.einsum('tbj,tzji->tzbi', win_re, band_im, precision=highest) + jnp.einsum('tbj,tzji->tzbi', win_im, band_re, precision=highest)
    return (out_re * out_re + out_im * out_im).reshape(trials, tmpl_re.shape[1], freq_count)

def reference(signal, tree_picks, tree_delays, template_bank, template_pick):
    channels, samples = signal.shape
    rim_depth = SECTIONS * MAXD
    extended = jnp.concatenate([signal, jnp.zeros((channels, rim_depth), signal.dtype)], axis=1)
    length = samples + rim_depth
    for section_num in range(SECTIONS):
        length = length - MAXD
        extended = group_section(extended, section_num, 0, tree_picks[0, section_num], tree_picks[1, section_num], tree_delays[section_num], length)
    norm_scale = 1.0 / math.sqrt(samples * channels)
    spectrum = jnp.fft.rfft(extended, axis=1)[:, :FREQS] * norm_scale
    spec_re = jnp.real(spectrum).astype(jnp.float32)
    spec_im = jnp.imag(spectrum).astype(jnp.float32)
    picked = template_pick.reshape(channels, ZSEL)
    tmpl_re = template_bank[0][picked]
    tmpl_im = template_bank[1][picked]
    group_size = 8
    group_count = channels // group_size

    def one_group(items):
        return template_powers(items[0], items[1], items[2], items[3])
    grouped = lax.map(one_group, (spec_re.reshape(group_count, group_size, FREQS), spec_im.reshape(group_count, group_size, FREQS), tmpl_re.reshape(group_count, group_size, ZSEL, TAPS), tmpl_im.reshape(group_count, group_size, ZSEL, TAPS)))
    return grouped.reshape(SUBBANDS, CH_DEV, ZSEL, FREQS)
```

```python
import functools
import math

import jax
import jax.numpy as jnp
import ml_dtypes
import numpy as np
from jax import lax
from jax.experimental import pallas as pl
from jax.experimental.pallas import tpu as pltpu
from jax.sharding import PartitionSpec as P

CH_DEV = 64
LOGCD = 6
MAXD = 4
LANES = 128
SUBS = 8
RADIX = 256
LIMIT = 56 * 1024 * 1024


def shifted(value, axis, steps):
    count = lax.axis_size(axis)
    first, last = (max(0, -steps), min(count, count - steps))
    return lax.ppermute(value, axis, [(source, source + steps) for source in range(first, last)])


def tree_kernel(sections, chunks, low_ref, high_ref, delay_ref, row_ref, x_ref, rim_ref, *rest):
    outs, (buf_a, buf_b) = rest[:chunks], rest[chunks:]
    rows, _, width = x_ref.shape
    tiles = width // LANES
    per = rows // chunks
    lane = lax.broadcasted_iota(jnp.int32, (SUBS, LANES), 1)
    sub = lax.broadcasted_iota(jnp.int32, (SUBS, LANES), 0)

    @pl.loop(0, rows, unroll=4)
    def _(r):
        head = x_ref[r, :, 0:LANES]
        buf_a[r, :, 0:width] = x_ref[r]
        up = pltpu.roll(head, SUBS - 1, 0)
        buf_a[r, :, width : width + LANES] = jnp.where(sub == SUBS - 1, rim_ref[r], up)

    def merge(src, section, r, dst, at, count):
        a = low_ref[section, r]
        b = high_ref[section, r]
        d = delay_ref[section, r]
        turn = lax.rem(LANES - d, LANES)
        keep = lane < LANES - d
        turned = [
            pltpu.roll(src[b, :, i * LANES : (i + 1) * LANES], turn, 1) for i in range(tiles + 1)
        ]
        for i in range(count):
            later = turned[min(i + 1, tiles)]
            dst[at, :, i * LANES : (i + 1) * LANES] = src[
                a, :, i * LANES : (i + 1) * LANES
            ] + jnp.where(keep, turned[i], later)

    src, dst = buf_a, buf_b
    for section in range(sections - 1):

        @pl.loop(0, rows, unroll=4)
        def _(r, src=src, dst=dst, section=section):
            merge(src, section, r, dst, r, tiles + 1)

        src, dst = dst, src
    for q in range(chunks):

        @pl.loop(0, per, unroll=4)
        def _(i, q=q, src=src):
            merge(src, sections - 1, row_ref[q, i], outs[q], i, tiles)


def tree(x, rim, low, high, delays, order):
    rows, _, width = x.shape
    chunks, per = order.shape
    sections = low.shape[0]
    smem = pl.BlockSpec(memory_space=pltpu.SMEM)
    vmem = pl.BlockSpec(memory_space=pltpu.VMEM)
    return pl.pallas_call(
        functools.partial(tree_kernel, sections, chunks),
        out_shape=[jax.ShapeDtypeStruct((per, SUBS, width), jnp.float32)] * chunks,
        in_specs=[smem] * 4 + [vmem] * 2,
        out_specs=[vmem] * chunks,
        scratch_shapes=[pltpu.VMEM((rows, SUBS, width + LANES), jnp.float32)] * 2,
        compiler_params=pltpu.CompilerParams(vmem_limit_bytes=LIMIT),
        cost_estimate=pl.CostEstimate(
            flops=rows * SUBS * width * sections * 4,
            bytes_accessed=rows * SUBS * width * 8,
            transcendentals=0,
        ),
        name="tree",
    )(low, high, delays, order, x, rim)


def split(value):
    high = value.astype(jnp.bfloat16)
    return high, (value - high.astype(jnp.float32)).astype(jnp.bfloat16)


def bands_kernel(zsel, u_ref, high_ref, low_ref):
    for z in range(zsel):
        pair = []
        for part in range(2):
            row = u_ref[0, 2 * z + part : 2 * z + part + 1, :]
            wide = jnp.broadcast_to(row, (RADIX, RADIX))
            band = pltpu.roll(wide, 0, 1, stride=1, stride_axis=0)[:, :LANES]
            pair.append(split(band))
        at = 2 * z * LANES
        for ref, real, imag in (
            (high_ref, pair[0][0], pair[1][0]),
            (low_ref, pair[0][1], pair[1][1]),
        ):
            ref[0, :RADIX, at : at + LANES] = real
            ref[0, RADIX:, at : at + LANES] = -imag
            ref[0, :RADIX, at + LANES : at + 2 * LANES] = imag
            ref[0, RADIX:, at + LANES : at + 2 * LANES] = real


def bands(picks, template_bank):
    trials, zsel = picks.shape
    taps = template_bank.shape[2]
    onehot = (picks[:, :, None] == jnp.arange(template_bank.shape[1], dtype=jnp.int32)).astype(
        jnp.float32
    )
    reversed_bank = jnp.concatenate(
        [
            template_bank[:, :, :1],
            jnp.zeros(template_bank.shape[:2] + (RADIX - taps,), jnp.float32),
            template_bank[:, :, :0:-1],
        ],
        axis=2,
    )
    u = jnp.einsum("tzk,ckm->tzcm", onehot, reversed_bank, precision=lax.Precision.HIGHEST)
    u = u.reshape(trials, 2 * zsel, RADIX)
    wide = 2 * zsel * LANES
    shape = jax.ShapeDtypeStruct((trials, 2 * RADIX, wide), jnp.bfloat16)
    spec = pl.BlockSpec((1, 2 * RADIX, wide), lambda t: (t, 0, 0))
    return pl.pallas_call(
        functools.partial(bands_kernel, zsel),
        grid=(trials,),
        out_shape=[shape, shape],
        in_specs=[pl.BlockSpec((1, 2 * zsel, RADIX), lambda t: (t, 0, 0))],
        out_specs=[spec, spec],
        compiler_params=pltpu.CompilerParams(vmem_limit_bytes=LIMIT),
        cost_estimate=pl.CostEstimate(
            flops=trials * RADIX * RADIX * 20,
            bytes_accessed=trials * 2 * RADIX * wide * 4,
            transcendentals=0,
        ),
        name="bands",
    )(u)


def tables(samples, channels, width, taps):
    cols = samples // RADIX
    outs = cols // 2
    split_by = width // cols if width % cols == 0 else 1
    place = np.arange(RADIX)
    row_of = split_by * (place % (RADIX // split_by)) + place // (RADIX // split_by)
    freq = (np.arange(RADIX) - taps // 2) % RADIX
    b = np.arange(cols)
    scale = 1.0 / math.sqrt(samples * channels)
    angle = 2.0 * np.pi / RADIX * (row_of[:, None] * freq[None, :] % RADIX)
    first = np.concatenate([np.cos(angle), -np.sin(angle)], axis=1) * scale
    angle = 2.0 * np.pi / samples * (b[:, None] * freq[None, :] % samples)
    tw_cos, tw_sin = np.cos(angle), np.sin(angle)
    angle = 2.0 * np.pi / cols * (np.arange(outs)[:, None] * b[None, :] % cols)
    second = np.concatenate([np.cos(angle), np.sin(angle)], axis=1)

    def parts(value):
        value = value.astype(np.float32)
        high = value.astype(ml_dtypes.bfloat16)
        return high, (value - high.astype(np.float32)).astype(ml_dtypes.bfloat16)

    return (
        *parts(first),
        tw_cos.astype(np.float32),
        tw_sin.astype(np.float32),
        *parts(second),
    )


def dot3(a_high, a_low, b_high, b_low):
    def dot(a, b):
        return jnp.dot(a, b, preferred_element_type=jnp.float32)

    return dot(a_high, b_high) + (dot(a_high, b_low) + dot(a_low, b_high))


def spectra_kernel(zsel, half_taps, aliased, *refs):
    x_ref, bh_ref, bl_ref, fh, fl, tc, ts, sh, sl = refs[:9]
    out_ref = refs[10] if aliased else refs[9]
    cols = tc.shape[0]
    outs = cols // 2
    x = x_ref[...]
    x = x.reshape(-1, x.shape[-1])
    if x.shape[1] != cols:
        x = jnp.concatenate(
            [x[:, i * cols : (i + 1) * cols] for i in range(x.shape[1] // cols)], axis=0
        )
    x_high, x_low = split(x.T)
    first = dot3(x_high, x_low, fh[...], fl[...])
    re, im = first[:, :RADIX], first[:, RADIX:]
    mid_re = re * tc[...] + im * ts[...]
    mid_im = im * tc[...] - re * ts[...]
    re_high, re_low = split(mid_re)
    im_high, im_low = split(mid_im)

    def block(a, b):
        return jnp.concatenate(
            [jnp.concatenate([a, b], axis=1), jnp.concatenate([b, -a], axis=1)], axis=0
        )

    spec = dot3(sh[...], sl[...], block(re_high, im_high), block(re_low, im_low))
    row = lax.broadcasted_iota(jnp.int32, (outs, RADIX), 0)
    lane = lax.broadcasted_iota(jnp.int32, (outs, RADIX), 1)
    even, odd = [], []
    for part in (spec[:, :RADIX], spec[:, RADIX:]):
        down = jnp.where(row == 0, 0.0, pltpu.roll(part, 1, 0))
        up = jnp.where(row == outs - 1, 0.0, pltpu.roll(part, outs - 1, 0))
        here = jnp.where(lane < half_taps, down, part)
        after = jnp.where(lane < half_taps, part, up)
        even.append(here)
        odd += [here[:, LANES:], after[:, :LANES]]
    window = jnp.concatenate(
        [jnp.concatenate(even, axis=1), jnp.concatenate(odd, axis=1)], axis=0
    )
    w_high, w_low = split(window)
    got = dot3(w_high, w_low, bh_ref[0], bl_ref[0])
    for z in range(zsel):
        at = 2 * z * LANES
        real, imag = got[:, at : at + LANES], got[:, at + LANES : at + 2 * LANES]
        power = real * real + imag * imag
        for e in range(2):
            out_ref[0, pl.ds(e * zsel + z, outs, 2 * zsel), :] = power[e * outs : (e + 1) * outs]


def spectra(x, band_high, band_low, consts, zsel, taps, trials, first_trial, so_far):
    cols = consts[2].shape[0]
    outs = cols // 2
    rows = 2 * outs * zsel
    if x.shape[-1] % cols == 0:
        here = x.shape[1]
        x_spec = pl.BlockSpec((x.shape[0], 1, SUBS, x.shape[-1]), lambda t: (0, t, 0, 0))
    else:
        here = x.shape[1]
        x = x.transpose(1, 0, 2, 3).reshape(here, RADIX, cols)
        x_spec = pl.BlockSpec((1, RADIX, cols), lambda t: (t, 0, 0))
    band_spec = pl.BlockSpec(
        (1,) + band_high.shape[1:], lambda t: (first_trial + t, 0, 0)
    )
    whole = [pl.BlockSpec(c.shape, lambda t: (0, 0)) for c in consts]
    aliased = so_far is not None
    more = [so_far] if aliased else []
    macs = here * (cols * RADIX * 2 * RADIX + outs * 2 * cols * 2 * RADIX + 2 * outs * 4 * RADIX * RADIX)
    return pl.pallas_call(
        functools.partial(spectra_kernel, zsel, taps // 2, aliased),
        grid=(here,),
        out_shape=jax.ShapeDtypeStruct((trials, rows, LANES), jnp.float32),
        in_specs=[x_spec, band_spec, band_spec, *whole]
        + [pl.BlockSpec(memory_space=pl.ANY)] * len(more),
        out_specs=pl.BlockSpec((1, rows, LANES), lambda t: (first_trial + t, 0, 0)),
        input_output_aliases={9: 0} if aliased else {},
        compiler_params=pltpu.CompilerParams(vmem_limit_bytes=LIMIT),
        cost_estimate=pl.CostEstimate(
            flops=6 * macs, bytes_accessed=here * 2 * 1024 * 1024, transcendentals=0
        ),
        name="spectra",
    )(x, band_high, band_low, *consts, *more)


def on_device(signal, tree_picks, tree_delays, template_bank, template_pick):
    band_count = lax.axis_size("band")
    time_count = lax.axis_size("tm")
    everyone = band_count * time_count
    sections = LOGCD + band_count.bit_length() - 1
    rim_depth = sections * MAXD
    channels = CH_DEV * band_count
    samples = signal.shape[1] * time_count
    slab = signal.shape[1] // band_count
    width = slab // SUBS
    trials = CH_DEV // time_count
    chunks = min(4, trials)
    zsel = template_pick.shape[2]
    taps = template_bank.shape[2]

    band_high, band_low = bands(template_pick[0], template_bank)

    folded = signal.reshape(CH_DEV, band_count, SUBS, width).transpose(1, 0, 2, 3)
    x = lax.all_to_all(folded, "band", split_axis=0, concat_axis=0, tiled=True)
    x = x.reshape(channels, SUBS, width)
    rim = shifted(x[:, 0, :rim_depth], ("tm", "band"), -1)
    rim = jnp.pad(rim, ((0, 0), (0, LANES - rim_depth)))
    rim = jnp.broadcast_to(rim[:, None, :], (channels, SUBS, LANES))

    half = (1 << np.arange(sections))[:, None]
    r = np.arange(channels)[None, :]
    base = r - r % (2 * half) + r % half - r % np.minimum(half, CH_DEV)
    low = tree_picks[0] + base.astype(np.int32)
    high = tree_picks[1] + (base + half).astype(np.int32)
    order = np.arange(channels).reshape(band_count, time_count, chunks, trials // chunks)
    order = order.transpose(2, 1, 0, 3).reshape(chunks, -1).astype(np.int32)
    pieces = tree(x, rim, low, high, tree_delays, jnp.asarray(order))

    consts = [jnp.asarray(c) for c in tables(samples, channels, width, taps)]
    out = None
    size = trials // chunks
    for q, piece in enumerate(pieces):
        piece = piece.reshape(everyone, size, SUBS, width)
        piece = lax.all_to_all(piece, ("tm", "band"), split_axis=0, concat_axis=0, tiled=True)
        out = spectra(piece, band_high, band_low, consts, zsel, taps, trials, q * size, out)
    out = out.reshape(trials, samples // 2 // LANES, zsel, LANES).transpose(0, 2, 1, 3)
    return out.reshape(1, trials, zsel, samples // 2)


def solution(mesh):
    in_specs = (P(("beams", "band"), "tm"), P(), P(), P(), P(("beams", "band"), "tm", None))
    out_specs = P(("beams", "band"), "tm", None, None)
    return jax.shard_map(
        on_device, mesh=mesh, in_specs=in_specs, out_specs=out_specs, check_vma=False
    )
```

```python
import functools
import math

import jax
import jax.numpy as jnp
import ml_dtypes
import numpy as np
from jax import lax
from jax.experimental import pallas as pl
from jax.experimental.pallas import tpu as pltpu
from jax.sharding import PartitionSpec as P

CH_DEV = 64
LOGCD = 6
MAXD = 4
LANES = 128
SUBS = 8
RADIX = 256
LIMIT = 56 * 1024 * 1024


def shifted(value, axis, steps):
    count = lax.axis_size(axis)
    first, last = (max(0, -steps), min(count, count - steps))
    return lax.ppermute(value, axis, [(source, source + steps) for source in range(first, last)])


def tree_kernel(sections, chunks, low_ref, high_ref, delay_ref, row_ref, x_ref, rim_ref, *rest):
    outs, (buf_a, buf_b) = rest[:chunks], rest[chunks:]
    rows, _, width = x_ref.shape
    tiles = width // LANES
    per = rows // chunks
    lane = lax.broadcasted_iota(jnp.int32, (SUBS, LANES), 1)
    sub = lax.broadcasted_iota(jnp.int32, (SUBS, LANES), 0)

    @pl.loop(0, rows, unroll=8)
    def _(r):
        head = x_ref[r, :, 0:LANES]
        buf_a[r, :, 0:width] = x_ref[r]
        up = pltpu.roll(head, SUBS - 1, 0)
        buf_a[r, :, width : width + LANES] = jnp.where(sub == SUBS - 1, rim_ref[r], up)

    def merge(src, section, r, dst, at, count):
        a = low_ref[section, r]
        b = high_ref[section, r]
        d = delay_ref[section, r]
        turn = (LANES - d) & (LANES - 1)
        keep = lane < LANES - d
        turned = [
            pltpu.roll(src[b, :, i * LANES : (i + 1) * LANES], turn, 1) for i in range(tiles + 1)
        ]
        for i in range(count):
            later = turned[min(i + 1, tiles)]
            dst[at, :, i * LANES : (i + 1) * LANES] = src[
                a, :, i * LANES : (i + 1) * LANES
            ] + jnp.where(keep, turned[i], later)

    src, dst = buf_a, buf_b
    for section in range(sections - 1):

        @pl.loop(0, rows, unroll=8)
        def _(r, src=src, dst=dst, section=section):
            merge(src, section, r, dst, r, tiles + 1)

        src, dst = dst, src
    for q in range(chunks):

        @pl.loop(0, per, unroll=8)
        def _(i, q=q, src=src):
            merge(src, sections - 1, row_ref[q, i], outs[q], i, tiles)


def tree(x, rim, low, high, delays, order):
    rows, _, width = x.shape
    chunks, per = order.shape
    sections = low.shape[0]
    smem = pl.BlockSpec(memory_space=pltpu.SMEM)
    vmem = pl.BlockSpec(memory_space=pltpu.VMEM)
    return pl.pallas_call(
        functools.partial(tree_kernel, sections, chunks),
        out_shape=[jax.ShapeDtypeStruct((per, SUBS, width), jnp.float32)] * chunks,
        in_specs=[smem] * 4 + [vmem] * 2,
        out_specs=[vmem] * chunks,
        scratch_shapes=[pltpu.VMEM((rows, SUBS, width + LANES), jnp.float32)] * 2,
        compiler_params=pltpu.CompilerParams(vmem_limit_bytes=LIMIT),
        cost_estimate=pl.CostEstimate(
            flops=rows * SUBS * width * sections * 4,
            bytes_accessed=rows * SUBS * width * 8,
            transcendentals=0,
        ),
        name="tree",
    )(low, high, delays, order, x, rim)


def split(value):
    high = value.astype(jnp.bfloat16)
    return high, (value - high.astype(jnp.float32)).astype(jnp.bfloat16)


def bands_kernel(zsel, u_ref, high_ref, low_ref):
    for z in range(zsel):
        pair = []
        for part in range(2):
            row = u_ref[0, 2 * z + part : 2 * z + part + 1, :]
            wide = jnp.broadcast_to(row, (RADIX, RADIX))
            band = pltpu.roll(wide, 0, 1, stride=1, stride_axis=0)[:, :LANES]
            pair.append(split(band))
        at = 2 * z * LANES
        for ref, real, imag in (
            (high_ref, pair[0][0], pair[1][0]),
            (low_ref, pair[0][1], pair[1][1]),
        ):
            ref[0, :RADIX, at : at + LANES] = real
            ref[0, RADIX:, at : at + LANES] = -imag
            ref[0, :RADIX, at + LANES : at + 2 * LANES] = imag
            ref[0, RADIX:, at + LANES : at + 2 * LANES] = real


def bands(picks, template_bank):
    trials, zsel = picks.shape
    taps = template_bank.shape[2]
    onehot = (picks[:, :, None] == jnp.arange(template_bank.shape[1], dtype=jnp.int32)).astype(
        jnp.float32
    )
    reversed_bank = jnp.concatenate(
        [
            template_bank[:, :, :1],
            jnp.zeros(template_bank.shape[:2] + (RADIX - taps,), jnp.float32),
            template_bank[:, :, :0:-1],
        ],
        axis=2,
    )
    u = jnp.einsum("tzk,ckm->tzcm", onehot, reversed_bank, precision=lax.Precision.HIGHEST)
    u = u.reshape(trials, 2 * zsel, RADIX)
    wide = 2 * zsel * LANES
    shape = jax.ShapeDtypeStruct((trials, 2 * RADIX, wide), jnp.bfloat16)
    spec = pl.BlockSpec((1, 2 * RADIX, wide), lambda t: (t, 0, 0))
    return pl.pallas_call(
        functools.partial(bands_kernel, zsel),
        grid=(trials,),
        out_shape=[shape, shape],
        in_specs=[pl.BlockSpec((1, 2 * zsel, RADIX), lambda t: (t, 0, 0))],
        out_specs=[spec, spec],
        compiler_params=pltpu.CompilerParams(vmem_limit_bytes=LIMIT),
        cost_estimate=pl.CostEstimate(
            flops=trials * RADIX * RADIX * 20,
            bytes_accessed=trials * 2 * RADIX * wide * 4,
            transcendentals=0,
        ),
        name="bands",
    )(u)


def tables(samples, channels, width, taps):
    cols = samples // RADIX
    outs = cols // 2
    split_by = width // cols if width % cols == 0 else 1
    place = np.arange(RADIX)
    row_of = split_by * (place % (RADIX // split_by)) + place // (RADIX // split_by)
    freq = (np.arange(RADIX) - taps // 2) % RADIX
    b = np.arange(cols)
    scale = 1.0 / math.sqrt(samples * channels)
    angle = 2.0 * np.pi / RADIX * (row_of[:, None] * freq[None, :] % RADIX)
    first = np.concatenate([np.cos(angle), -np.sin(angle)], axis=1) * scale
    angle = 2.0 * np.pi / samples * (b[:, None] * freq[None, :] % samples)
    tw_cos, tw_sin = np.cos(angle), np.sin(angle)
    angle = 2.0 * np.pi / cols * (np.arange(outs)[:, None] * b[None, :] % cols)
    second = np.concatenate([np.cos(angle), np.sin(angle)], axis=1)

    def parts(value):
        value = value.astype(np.float32)
        high = value.astype(ml_dtypes.bfloat16)
        return high, (value - high.astype(np.float32)).astype(ml_dtypes.bfloat16)

    return (
        *parts(first),
        tw_cos.astype(np.float32),
        tw_sin.astype(np.float32),
        *parts(second),
    )


def dot3(a_high, a_low, b_high, b_low):
    def dot(a, b):
        return jnp.dot(a, b, preferred_element_type=jnp.float32)

    return dot(a_high, b_high) + (dot(a_high, b_low) + dot(a_low, b_high))


def spectra_kernel(zsel, half_taps, aliased, *refs):
    x_ref, bh_ref, bl_ref, fh, fl, tc, ts, sh, sl = refs[:9]
    out_ref, done_ref = refs[10:] if aliased else refs[9:]
    done_ref[...] = jnp.zeros_like(done_ref)
    cols = tc.shape[0]
    outs = cols // 2
    x = x_ref[...]
    x = x.reshape(-1, x.shape[-1])
    if x.shape[1] != cols:
        x = jnp.concatenate(
            [x[:, i * cols : (i + 1) * cols] for i in range(x.shape[1] // cols)], axis=0
        )
    x_high, x_low = split(x.T)
    first = dot3(x_high, x_low, fh[...], fl[...])
    re, im = first[:, :RADIX], first[:, RADIX:]
    mid_re = re * tc[...] + im * ts[...]
    mid_im = im * tc[...] - re * ts[...]
    re_high, re_low = split(mid_re)
    im_high, im_low = split(mid_im)

    def block(a, b):
        return jnp.concatenate(
            [jnp.concatenate([a, b], axis=1), jnp.concatenate([b, -a], axis=1)], axis=0
        )

    spec = dot3(sh[...], sl[...], block(re_high, im_high), block(re_low, im_low))
    row = lax.broadcasted_iota(jnp.int32, (outs, RADIX), 0)
    lane = lax.broadcasted_iota(jnp.int32, (outs, RADIX), 1)
    even, odd = [], []
    for part in (spec[:, :RADIX], spec[:, RADIX:]):
        down = jnp.where(row == 0, 0.0, pltpu.roll(part, 1, 0))
        up = jnp.where(row == outs - 1, 0.0, pltpu.roll(part, outs - 1, 0))
        here = jnp.where(lane < half_taps, down, part)
        after = jnp.where(lane < half_taps, part, up)
        even.append(here)
        odd += [here[:, LANES:], after[:, :LANES]]
    window = jnp.concatenate(
        [jnp.concatenate(even, axis=1), jnp.concatenate(odd, axis=1)], axis=0
    )
    w_high, w_low = split(window)
    got = dot3(w_high, w_low, bh_ref[0], bl_ref[0])
    for z in range(zsel):
        at = 2 * z * LANES
        real, imag = got[:, at : at + LANES], got[:, at + LANES : at + 2 * LANES]
        power = real * real + imag * imag
        for e in range(2):
            out_ref[0, pl.ds(e * zsel + z, outs, 2 * zsel), :] = power[e * outs : (e + 1) * outs]


def spectra(x, band_high, band_low, consts, zsel, taps, trials, first_trial, so_far):
    cols = consts[2].shape[0]
    outs = cols // 2
    rows = 2 * outs * zsel
    if x.shape[-1] % cols == 0:
        here = x.shape[1]
        x_spec = pl.BlockSpec((x.shape[0], 1, SUBS, x.shape[-1]), lambda t: (0, t, 0, 0))
    else:
        here = x.shape[1]
        x = x.transpose(1, 0, 2, 3).reshape(here, RADIX, cols)
        x_spec = pl.BlockSpec((1, RADIX, cols), lambda t: (t, 0, 0))
    band_spec = pl.BlockSpec(
        (1,) + band_high.shape[1:], lambda t: (first_trial + t, 0, 0)
    )
    whole = [pl.BlockSpec(c.shape, lambda t: (0, 0)) for c in consts]
    aliased = so_far is not None
    more = [so_far] if aliased else []
    macs = here * (cols * RADIX * 2 * RADIX + outs * 2 * cols * 2 * RADIX + 2 * outs * 4 * RADIX * RADIX)
    return pl.pallas_call(
        functools.partial(spectra_kernel, zsel, taps // 2, aliased),
        grid=(here,),
        out_shape=[
            jax.ShapeDtypeStruct((trials, rows, LANES), jnp.float32),
            jax.ShapeDtypeStruct((SUBS, LANES), jnp.float32),
        ],
        in_specs=[x_spec, band_spec, band_spec, *whole]
        + [pl.BlockSpec(memory_space=pl.ANY)] * len(more),
        out_specs=[
            pl.BlockSpec((1, rows, LANES), lambda t: (first_trial + t, 0, 0)),
            pl.BlockSpec((SUBS, LANES), lambda t: (0, 0)),
        ],
        input_output_aliases={9: 0} if aliased else {},
        compiler_params=pltpu.CompilerParams(vmem_limit_bytes=LIMIT),
        cost_estimate=pl.CostEstimate(
            flops=6 * macs, bytes_accessed=here * 2 * 1024 * 1024, transcendentals=0
        ),
        name="spectra",
    )(x, band_high, band_low, *consts, *more)


def after_kernel(value_ref, done_ref, out_ref):
    del value_ref, done_ref, out_ref


def after(value, done):
    anywhere = pl.BlockSpec(memory_space=pl.ANY)
    return pl.pallas_call(
        after_kernel,
        out_shape=jax.ShapeDtypeStruct(value.shape, value.dtype),
        in_specs=[anywhere, anywhere],
        out_specs=anywhere,
        input_output_aliases={0: 0},
        name="after",
    )(value, done)


def on_device(signal, tree_picks, tree_delays, template_bank, template_pick):
    band_count = lax.axis_size("band")
    time_count = lax.axis_size("tm")
    everyone = band_count * time_count
    sections = LOGCD + band_count.bit_length() - 1
    rim_depth = sections * MAXD
    channels = CH_DEV * band_count
    samples = signal.shape[1] * time_count
    slab = signal.shape[1] // band_count
    width = slab // SUBS
    trials = CH_DEV // time_count
    chunks = min(4, trials)
    zsel = template_pick.shape[2]
    taps = template_bank.shape[2]

    band_high, band_low = bands(template_pick[0], template_bank)

    folded = signal.reshape(CH_DEV, band_count, SUBS, width).transpose(1, 0, 2, 3)
    x = lax.all_to_all(folded, "band", split_axis=0, concat_axis=0, tiled=True)
    x = x.reshape(channels, SUBS, width)
    rim = shifted(x[:, 0, :rim_depth], ("tm", "band"), -1)
    rim = jnp.pad(rim, ((0, 0), (0, LANES - rim_depth)))
    rim = jnp.broadcast_to(rim[:, None, :], (channels, SUBS, LANES))

    half = (1 << np.arange(sections))[:, None]
    r = np.arange(channels)[None, :]
    base = r - r % (2 * half) + r % half - r % np.minimum(half, CH_DEV)
    low = tree_picks[0] + base.astype(np.int32)
    high = tree_picks[1] + (base + half).astype(np.int32)
    order = np.arange(channels).reshape(band_count, time_count, chunks, trials // chunks)
    order = order.transpose(2, 1, 0, 3).reshape(chunks, -1).astype(np.int32)
    pieces = tree(x, rim, low, high, tree_delays, jnp.asarray(order))

    consts = [jnp.asarray(c) for c in tables(samples, channels, width, taps)]
    out = None
    size = trials // chunks
    dones = []
    for q, piece in enumerate(pieces):
        if q >= 2:
            piece = after(piece, dones[q - 2])
        piece = piece.reshape(everyone, size, SUBS, width)
        piece = lax.all_to_all(piece, ("tm", "band"), split_axis=0, concat_axis=0, tiled=True)
        out, done = spectra(piece, band_high, band_low, consts, zsel, taps, trials, q * size, out)
        dones.append(done)
    out = out.reshape(trials, samples // 2 // LANES, zsel, LANES).transpose(0, 2, 1, 3)
    return out.reshape(1, trials, zsel, samples // 2)


def solution(mesh):
    in_specs = (P(("beams", "band"), "tm"), P(), P(), P(), P(("beams", "band"), "tm", None))
    out_specs = P(("beams", "band"), "tm", None, None)
    return jax.shard_map(
        on_device, mesh=mesh, in_specs=in_specs, out_specs=out_specs, check_vma=False
    )
```

```python
import functools
import math

import jax
import jax.numpy as jnp
import ml_dtypes
import numpy as np
from jax import lax
from jax.experimental import pallas as pl
from jax.experimental.pallas import tpu as pltpu
from jax.sharding import PartitionSpec as P

CH_DEV = 64
LOGCD = 6
MAXD = 4
LANES = 128
SUBS = 8
RADIX = 256
LIMIT = 56 * 1024 * 1024


def shifted(value, axis, steps):
    count = lax.axis_size(axis)
    first, last = (max(0, -steps), min(count, count - steps))
    return lax.ppermute(value, axis, [(source, source + steps) for source in range(first, last)])


def tree_kernel(sections, sizes, parts, has_rim, *refs):
    low_ref, high_ref, delay_ref, row_ref = refs[:4]
    xs, refs = refs[4 : 4 + len(parts)], refs[4 + len(parts) :]
    if has_rim:
        rim_ref, refs = refs[0], refs[1:]
    buf_a, buf_b = refs[-2:]
    outs = refs[len(refs) - 2 - len(sizes) : -2]
    rows, _, span = buf_a.shape
    tiles = span // LANES - 1
    lane = lax.broadcasted_iota(jnp.int32, (SUBS, LANES), 1)
    sub = lax.broadcasted_iota(jnp.int32, (SUBS, LANES), 0)

    @pl.loop(0, rows, unroll=4)
    def _(r):
        at = 0
        for x_ref, first in zip(xs, parts):
            count = x_ref.shape[2] - first
            buf_a[r, :, at : at + count] = x_ref[r, :, first:]
            at += count
        if has_rim:
            up = pltpu.roll(xs[0][r, :, 0:LANES], SUBS - 1, 0)
            buf_a[r, :, at : at + LANES] = jnp.where(sub == SUBS - 1, rim_ref[r], up)

    def merge(src, section, r, dst, at, count):
        a = low_ref[section, r]
        b = high_ref[section, r]
        d = delay_ref[section, r]
        turn = (LANES - d) & (LANES - 1)
        keep = lane < LANES - d
        turned = [
            pltpu.roll(src[b, :, i * LANES : (i + 1) * LANES], turn, 1) for i in range(tiles + 1)
        ]
        for i in range(count):
            later = turned[min(i + 1, tiles)]
            dst[at, :, i * LANES : (i + 1) * LANES] = src[
                a, :, i * LANES : (i + 1) * LANES
            ] + jnp.where(keep, turned[i], later)

    src, dst = buf_a, buf_b
    for section in range(sections - 1):

        @pl.loop(0, rows, unroll=8)
        def _(r, src=src, dst=dst, section=section):
            merge(src, section, r, dst, r, tiles + 1)

        src, dst = dst, src
    start = 0
    for size, out in zip(sizes, outs):

        @pl.loop(0, size, unroll=8)
        def _(i, start=start, src=src, out=out):
            merge(src, sections - 1, row_ref[start + i], out, i, tiles)

        start += size


def tree(xs, parts, rim, tables_of, sizes, width, span, place, so_far):
    rows = xs[0].shape[0]
    sections = tables_of[0].shape[0]
    smem = pl.BlockSpec(memory_space=pltpu.SMEM)
    vmem = pl.BlockSpec(memory_space=pltpu.VMEM)
    has_rim = rim is not None
    inputs = [*tables_of, *xs] + ([rim] if has_rim else [])
    known = len(inputs)
    return pl.pallas_call(
        functools.partial(tree_kernel, sections, sizes, parts, has_rim),
        grid=(1,),
        out_shape=[jax.ShapeDtypeStruct((size, SUBS, width), jnp.float32) for size in sizes],
        in_specs=[smem] * 4
        + [vmem] * (known - 4)
        + [pl.BlockSpec(memory_space=pl.ANY)] * len(so_far),
        out_specs=[pl.BlockSpec((size, SUBS, span), lambda i: (0, 0, place)) for size in sizes],
        input_output_aliases={known + i: i for i in range(len(so_far))},
        scratch_shapes=[pltpu.VMEM((rows, SUBS, span + LANES), jnp.float32)] * 2,
        compiler_params=pltpu.CompilerParams(vmem_limit_bytes=LIMIT),
        cost_estimate=pl.CostEstimate(
            flops=rows * SUBS * span * sections * 4,
            bytes_accessed=rows * SUBS * span * 8,
            transcendentals=0,
        ),
        name="tree",
    )(*inputs, *so_far)


def split(value):
    high = value.astype(jnp.bfloat16)
    return high, (value - high.astype(jnp.float32)).astype(jnp.bfloat16)


def bands_kernel(zsel, u_ref, high_ref, low_ref):
    for z in range(zsel):
        pair = []
        for part in range(2):
            row = u_ref[0, 2 * z + part : 2 * z + part + 1, :]
            wide = jnp.broadcast_to(row, (RADIX, RADIX))
            band = pltpu.roll(wide, 0, 1, stride=1, stride_axis=0)[:, :LANES]
            pair.append(split(band))
        at = 2 * z * LANES
        for ref, real, imag in (
            (high_ref, pair[0][0], pair[1][0]),
            (low_ref, pair[0][1], pair[1][1]),
        ):
            ref[0, :RADIX, at : at + LANES] = real
            ref[0, RADIX:, at : at + LANES] = -imag
            ref[0, :RADIX, at + LANES : at + 2 * LANES] = imag
            ref[0, RADIX:, at + LANES : at + 2 * LANES] = real


def bands(picks, template_bank):
    trials, zsel = picks.shape
    taps = template_bank.shape[2]
    onehot = (picks[:, :, None] == jnp.arange(template_bank.shape[1], dtype=jnp.int32)).astype(
        jnp.float32
    )
    reversed_bank = jnp.concatenate(
        [
            template_bank[:, :, :1],
            jnp.zeros(template_bank.shape[:2] + (RADIX - taps,), jnp.float32),
            template_bank[:, :, :0:-1],
        ],
        axis=2,
    )
    u = jnp.einsum("tzk,ckm->tzcm", onehot, reversed_bank, precision=lax.Precision.HIGHEST)
    u = u.reshape(trials, 2 * zsel, RADIX)
    wide = 2 * zsel * LANES
    shape = jax.ShapeDtypeStruct((trials, 2 * RADIX, wide), jnp.bfloat16)
    spec = pl.BlockSpec((1, 2 * RADIX, wide), lambda t: (t, 0, 0))
    return pl.pallas_call(
        functools.partial(bands_kernel, zsel),
        grid=(trials,),
        out_shape=[shape, shape],
        in_specs=[pl.BlockSpec((1, 2 * zsel, RADIX), lambda t: (t, 0, 0))],
        out_specs=[spec, spec],
        compiler_params=pltpu.CompilerParams(vmem_limit_bytes=LIMIT),
        cost_estimate=pl.CostEstimate(
            flops=trials * RADIX * RADIX * 20,
            bytes_accessed=trials * 2 * RADIX * wide * 4,
            transcendentals=0,
        ),
        name="bands",
    )(u)


def tables(samples, channels, width, taps):
    cols = samples // RADIX
    outs = cols // 2
    split_by = width // cols if width % cols == 0 else 1
    place = np.arange(RADIX)
    row_of = split_by * (place % (RADIX // split_by)) + place // (RADIX // split_by)
    freq = (np.arange(RADIX) - taps // 2) % RADIX
    b = np.arange(cols)
    scale = 1.0 / math.sqrt(samples * channels)
    angle = 2.0 * np.pi / RADIX * (row_of[:, None] * freq[None, :] % RADIX)
    first = np.concatenate([np.cos(angle), -np.sin(angle)], axis=1) * scale
    angle = 2.0 * np.pi / samples * (b[:, None] * freq[None, :] % samples)
    tw_cos, tw_sin = np.cos(angle), np.sin(angle)
    angle = 2.0 * np.pi / cols * (np.arange(outs)[:, None] * b[None, :] % cols)
    second = np.concatenate([np.cos(angle), np.sin(angle)], axis=1)

    def parts(value):
        value = value.astype(np.float32)
        high = value.astype(ml_dtypes.bfloat16)
        return high, (value - high.astype(np.float32)).astype(ml_dtypes.bfloat16)

    return (
        *parts(first),
        tw_cos.astype(np.float32),
        tw_sin.astype(np.float32),
        *parts(second),
    )


def dot3(a_high, a_low, b_high, b_low):
    def dot(a, b):
        return jnp.dot(a, b, preferred_element_type=jnp.float32)

    return dot(a_high, b_high) + (dot(a_high, b_low) + dot(a_low, b_high))


def spectra_kernel(zsel, half_taps, aliased, *refs):
    x_ref, bh_ref, bl_ref, fh, fl, tc, ts, sh, sl = refs[:9]
    out_ref, done_ref = refs[10:] if aliased else refs[9:]
    done_ref[...] = jnp.zeros_like(done_ref)
    cols = tc.shape[0]
    outs = cols // 2
    x = x_ref[...]
    x = x.reshape(-1, x.shape[-1])
    if x.shape[1] != cols:
        x = jnp.concatenate(
            [x[:, i * cols : (i + 1) * cols] for i in range(x.shape[1] // cols)], axis=0
        )
    x_high, x_low = split(x.T)
    first = dot3(x_high, x_low, fh[...], fl[...])
    re, im = first[:, :RADIX], first[:, RADIX:]
    mid_re = re * tc[...] + im * ts[...]
    mid_im = im * tc[...] - re * ts[...]
    re_high, re_low = split(mid_re)
    im_high, im_low = split(mid_im)

    def block(a, b):
        return jnp.concatenate(
            [jnp.concatenate([a, b], axis=1), jnp.concatenate([b, -a], axis=1)], axis=0
        )

    spec = dot3(sh[...], sl[...], block(re_high, im_high), block(re_low, im_low))
    row = lax.broadcasted_iota(jnp.int32, (outs, RADIX), 0)
    lane = lax.broadcasted_iota(jnp.int32, (outs, RADIX), 1)
    even, odd = [], []
    for part in (spec[:, :RADIX], spec[:, RADIX:]):
        down = jnp.where(row == 0, 0.0, pltpu.roll(part, 1, 0))
        up = jnp.where(row == outs - 1, 0.0, pltpu.roll(part, outs - 1, 0))
        here = jnp.where(lane < half_taps, down, part)
        after = jnp.where(lane < half_taps, part, up)
        even.append(here)
        odd += [here[:, LANES:], after[:, :LANES]]
    window = jnp.concatenate(
        [jnp.concatenate(even, axis=1), jnp.concatenate(odd, axis=1)], axis=0
    )
    w_high, w_low = split(window)
    got = dot3(w_high, w_low, bh_ref[0], bl_ref[0])
    for z in range(zsel):
        at = 2 * z * LANES
        real, imag = got[:, at : at + LANES], got[:, at + LANES : at + 2 * LANES]
        power = real * real + imag * imag
        for e in range(2):
            out_ref[0, pl.ds(e * zsel + z, outs, 2 * zsel), :] = power[e * outs : (e + 1) * outs]


def spectra(x, band_high, band_low, consts, zsel, taps, trials, first_trial, so_far):
    cols = consts[2].shape[0]
    outs = cols // 2
    rows = 2 * outs * zsel
    if x.shape[-1] % cols == 0:
        here = x.shape[1]
        x_spec = pl.BlockSpec((x.shape[0], 1, SUBS, x.shape[-1]), lambda t: (0, t, 0, 0))
    else:
        here = x.shape[1]
        x = x.transpose(1, 0, 2, 3).reshape(here, RADIX, cols)
        x_spec = pl.BlockSpec((1, RADIX, cols), lambda t: (t, 0, 0))
    band_spec = pl.BlockSpec(
        (1,) + band_high.shape[1:], lambda t: (first_trial + t, 0, 0)
    )
    whole = [pl.BlockSpec(c.shape, lambda t: (0, 0)) for c in consts]
    aliased = so_far is not None
    more = [so_far] if aliased else []
    macs = here * (cols * RADIX * 2 * RADIX + outs * 2 * cols * 2 * RADIX + 2 * outs * 4 * RADIX * RADIX)
    return pl.pallas_call(
        functools.partial(spectra_kernel, zsel, taps // 2, aliased),
        grid=(here,),
        out_shape=[
            jax.ShapeDtypeStruct((trials, rows, LANES), jnp.float32),
            jax.ShapeDtypeStruct((SUBS, LANES), jnp.float32),
        ],
        in_specs=[x_spec, band_spec, band_spec, *whole]
        + [pl.BlockSpec(memory_space=pl.ANY)] * len(more),
        out_specs=[
            pl.BlockSpec((1, rows, LANES), lambda t: (first_trial + t, 0, 0)),
            pl.BlockSpec((SUBS, LANES), lambda t: (0, 0)),
        ],
        input_output_aliases={9: 0} if aliased else {},
        compiler_params=pltpu.CompilerParams(vmem_limit_bytes=LIMIT),
        cost_estimate=pl.CostEstimate(
            flops=6 * macs, bytes_accessed=here * 2 * 1024 * 1024, transcendentals=0
        ),
        name="spectra",
    )(x, band_high, band_low, *consts, *more)


def after_kernel(value_ref, done_ref, out_ref):
    del value_ref, done_ref, out_ref


def after(value, done):
    anywhere = pl.BlockSpec(memory_space=pl.ANY)
    return pl.pallas_call(
        after_kernel,
        out_shape=jax.ShapeDtypeStruct(value.shape, value.dtype),
        in_specs=[anywhere, anywhere],
        out_specs=anywhere,
        input_output_aliases={0: 0},
        name="after",
    )(value, done)


def on_device(signal, tree_picks, tree_delays, template_bank, template_pick):
    band_count = lax.axis_size("band")
    time_count = lax.axis_size("tm")
    everyone = band_count * time_count
    sections = LOGCD + band_count.bit_length() - 1
    rim_depth = sections * MAXD
    channels = CH_DEV * band_count
    samples = signal.shape[1] * time_count
    slab = signal.shape[1] // band_count
    width = slab // SUBS
    trials = CH_DEV // time_count
    last = max(1, trials // 4)
    counts = [count for count in (trials - last, last) if count]
    zsel = template_pick.shape[2]
    taps = template_bank.shape[2]

    band_high, band_low = bands(template_pick[0], template_bank)

    half = (1 << np.arange(sections))[:, None]
    r = np.arange(channels)[None, :]
    base = r - r % (2 * half) + r % half - r % np.minimum(half, CH_DEV)
    low = tree_picks[0] + base.astype(np.int32)
    high = tree_picks[1] + (base + half).astype(np.int32)
    grid = np.arange(channels).reshape(band_count, time_count, trials).transpose(1, 0, 2)
    firsts = [sum(counts[:q]) for q in range(len(counts))]
    order = np.concatenate(
        [grid[:, :, first : first + count].reshape(-1) for first, count in zip(firsts, counts)]
    ).astype(np.int32)
    tables_of = (low, high, tree_delays, jnp.asarray(order))
    sizes = [everyone * count for count in counts]

    folded = signal.reshape(CH_DEV, band_count, SUBS, width)

    def exchanged(value):
        value = lax.all_to_all(value, "band", split_axis=0, concat_axis=0, tiled=True)
        return value.reshape(channels, SUBS, -1)

    def rim_of(x):
        rim = shifted(x[:, 0, :rim_depth], ("tm", "band"), -1)
        rim = jnp.pad(rim, ((0, 0), (0, LANES - rim_depth)))
        return jnp.broadcast_to(rim[:, None, :], (channels, SUBS, LANES))

    if width % (2 * LANES) == 0:
        span = width // 2
        cut = span + LANES
        x_a = exchanged(folded[..., :cut].transpose(1, 0, 2, 3))
        x_b = exchanged(after(folded[..., cut:].transpose(1, 0, 2, 3), x_a))
        pieces = tree([x_a], [0], None, tables_of, sizes, width, span, 0, [])
        pieces = tree(
            [x_a, x_b], [span, 0], rim_of(x_a), tables_of, sizes, width, span, 1, pieces
        )
    else:
        x = exchanged(folded.transpose(1, 0, 2, 3))
        pieces = tree([x], [0], rim_of(x), tables_of, sizes, width, width, 0, [])

    consts = [jnp.asarray(c) for c in tables(samples, channels, width, taps)]
    out = None
    for first, count, piece in zip(firsts, counts, pieces):
        piece = piece.reshape(everyone, count, SUBS, width)
        if out is not None:
            piece = after(piece, arrived)
        arrived = lax.all_to_all(piece, ("tm", "band"), split_axis=0, concat_axis=0, tiled=True)
        out, _ = spectra(
            arrived, band_high, band_low, consts, zsel, taps, trials, first, out
        )
    out = out.reshape(trials, samples // 2 // LANES, zsel, LANES).transpose(0, 2, 1, 3)
    return out.reshape(1, trials, zsel, samples // 2)


def solution(mesh):
    in_specs = (P(("beams", "band"), "tm"), P(), P(), P(), P(("beams", "band"), "tm", None))
    out_specs = P(("beams", "band"), "tm", None, None)
    return jax.shard_map(
        on_device, mesh=mesh, in_specs=in_specs, out_specs=out_specs, check_vma=False
    )
```

```python
import functools
import math

import jax
import jax.numpy as jnp
import ml_dtypes
import numpy as np
from jax import lax
from jax.experimental import pallas as pl
from jax.experimental.pallas import tpu as pltpu
from jax.sharding import PartitionSpec as P

CH_DEV = 64
LOGCD = 6
MAXD = 4
LANES = 128
SUBS = 8
RADIX = 256
LIMIT = 56 * 1024 * 1024


def shifted(value, axis, steps):
    count = lax.axis_size(axis)
    first, last = (max(0, -steps), min(count, count - steps))
    return lax.ppermute(value, axis, [(source, source + steps) for source in range(first, last)])


def tree_kernel(sections, sizes, parts, has_rim, *refs):
    low_ref, high_ref, delay_ref, row_ref = refs[:4]
    xs, refs = refs[4 : 4 + len(parts)], refs[4 + len(parts) :]
    if has_rim:
        rim_ref, refs = refs[0], refs[1:]
    buf_a, buf_b = refs[-2:]
    outs = refs[len(refs) - 2 - len(sizes) : -2]
    rows, _, span = buf_a.shape
    tiles = span // LANES - 1
    lane = lax.broadcasted_iota(jnp.int32, (SUBS, LANES), 1)
    sub = lax.broadcasted_iota(jnp.int32, (SUBS, LANES), 0)

    @pl.loop(0, rows, unroll=4)
    def _(r):
        at = 0
        for x_ref, first in zip(xs, parts):
            count = x_ref.shape[2] - first
            buf_a[r, :, at : at + count] = x_ref[r, :, first:]
            at += count
        if has_rim:
            up = pltpu.roll(xs[0][r, :, 0:LANES], SUBS - 1, 0)
            buf_a[r, :, at : at + LANES] = jnp.where(sub == SUBS - 1, rim_ref[r], up)

    def merge(src, section, r, dst, at, count):
        a = low_ref[section, r]
        b = high_ref[section, r]
        d = delay_ref[section, r]
        turn = (LANES - d) & (LANES - 1)
        keep = lane < LANES - d
        turned = [
            pltpu.roll(src[b, :, i * LANES : (i + 1) * LANES], turn, 1) for i in range(tiles + 1)
        ]
        for i in range(count):
            later = turned[min(i + 1, tiles)]
            dst[at, :, i * LANES : (i + 1) * LANES] = src[
                a, :, i * LANES : (i + 1) * LANES
            ] + jnp.where(keep, turned[i], later)

    src, dst = buf_a, buf_b
    for section in range(sections - 1):

        @pl.loop(0, rows, unroll=16)
        def _(r, src=src, dst=dst, section=section):
            merge(src, section, r, dst, r, tiles + 1)

        src, dst = dst, src
    start = 0
    for size, out in zip(sizes, outs):

        @pl.loop(0, size, unroll=16)
        def _(i, start=start, src=src, out=out):
            merge(src, sections - 1, row_ref[start + i], out, i, tiles)

        start += size


def tree(xs, parts, rim, tables_of, sizes, width, span, place, so_far):
    rows = xs[0].shape[0]
    sections = tables_of[0].shape[0]
    smem = pl.BlockSpec(memory_space=pltpu.SMEM)
    vmem = pl.BlockSpec(memory_space=pltpu.VMEM)
    has_rim = rim is not None
    inputs = [*tables_of, *xs] + ([rim] if has_rim else [])
    known = len(inputs)
    return pl.pallas_call(
        functools.partial(tree_kernel, sections, sizes, parts, has_rim),
        grid=(1,),
        out_shape=[jax.ShapeDtypeStruct((size, SUBS, width), jnp.float32) for size in sizes],
        in_specs=[smem] * 4
        + [vmem] * (known - 4)
        + [pl.BlockSpec(memory_space=pl.ANY)] * len(so_far),
        out_specs=[pl.BlockSpec((size, SUBS, span), lambda i: (0, 0, place)) for size in sizes],
        input_output_aliases={known + i: i for i in range(len(so_far))},
        scratch_shapes=[pltpu.VMEM((rows, SUBS, span + LANES), jnp.float32)] * 2,
        compiler_params=pltpu.CompilerParams(vmem_limit_bytes=LIMIT),
        cost_estimate=pl.CostEstimate(
            flops=rows * SUBS * span * sections * 4,
            bytes_accessed=rows * SUBS * span * 8,
            transcendentals=0,
        ),
        name="tree",
    )(*inputs, *so_far)


def split(value):
    high = value.astype(jnp.bfloat16)
    return high, (value - high.astype(jnp.float32)).astype(jnp.bfloat16)


def bands_kernel(zsel, u_ref, high_ref, low_ref):
    for z in range(zsel):
        pair = []
        for part in range(2):
            row = u_ref[0, 2 * z + part : 2 * z + part + 1, :]
            wide = jnp.broadcast_to(row, (RADIX, RADIX))
            band = pltpu.roll(wide, 0, 1, stride=1, stride_axis=0)[:, :LANES]
            pair.append(split(band))
        at = 2 * z * LANES
        for ref, real, imag in (
            (high_ref, pair[0][0], pair[1][0]),
            (low_ref, pair[0][1], pair[1][1]),
        ):
            ref[0, :RADIX, at : at + LANES] = real
            ref[0, RADIX:, at : at + LANES] = -imag
            ref[0, :RADIX, at + LANES : at + 2 * LANES] = imag
            ref[0, RADIX:, at + LANES : at + 2 * LANES] = real


def bands(picks, template_bank):
    trials, zsel = picks.shape
    taps = template_bank.shape[2]
    onehot = (picks[:, :, None] == jnp.arange(template_bank.shape[1], dtype=jnp.int32)).astype(
        jnp.float32
    )
    reversed_bank = jnp.concatenate(
        [
            template_bank[:, :, :1],
            jnp.zeros(template_bank.shape[:2] + (RADIX - taps,), jnp.float32),
            template_bank[:, :, :0:-1],
        ],
        axis=2,
    )
    u = jnp.einsum("tzk,ckm->tzcm", onehot, reversed_bank, precision=lax.Precision.HIGHEST)
    u = u.reshape(trials, 2 * zsel, RADIX)
    wide = 2 * zsel * LANES
    shape = jax.ShapeDtypeStruct((trials, 2 * RADIX, wide), jnp.bfloat16)
    spec = pl.BlockSpec((1, 2 * RADIX, wide), lambda t: (t, 0, 0))
    return pl.pallas_call(
        functools.partial(bands_kernel, zsel),
        grid=(trials,),
        out_shape=[shape, shape],
        in_specs=[pl.BlockSpec((1, 2 * zsel, RADIX), lambda t: (t, 0, 0))],
        out_specs=[spec, spec],
        compiler_params=pltpu.CompilerParams(vmem_limit_bytes=LIMIT),
        cost_estimate=pl.CostEstimate(
            flops=trials * RADIX * RADIX * 20,
            bytes_accessed=trials * 2 * RADIX * wide * 4,
            transcendentals=0,
        ),
        name="bands",
    )(u)


def tables(samples, channels, width, taps):
    cols = samples // RADIX
    outs = cols // 2
    split_by = width // cols if width % cols == 0 else 1
    place = np.arange(RADIX)
    row_of = split_by * (place % (RADIX // split_by)) + place // (RADIX // split_by)
    freq = (np.arange(RADIX) - taps // 2) % RADIX
    b = np.arange(cols)
    scale = 1.0 / math.sqrt(samples * channels)
    angle = 2.0 * np.pi / RADIX * (row_of[:, None] * freq[None, :] % RADIX)
    first = np.concatenate([np.cos(angle), -np.sin(angle)], axis=1) * scale
    angle = 2.0 * np.pi / samples * (b[:, None] * freq[None, :] % samples)
    tw_cos, tw_sin = np.cos(angle), np.sin(angle)
    angle = 2.0 * np.pi / cols * (np.arange(outs)[:, None] * b[None, :] % cols)
    second = np.concatenate([np.cos(angle), np.sin(angle)], axis=1)

    def parts(value):
        value = value.astype(np.float32)
        high = value.astype(ml_dtypes.bfloat16)
        return high, (value - high.astype(np.float32)).astype(ml_dtypes.bfloat16)

    return (
        *parts(first),
        tw_cos.astype(np.float32),
        tw_sin.astype(np.float32),
        *parts(second),
    )


def dot3(a_high, a_low, b_high, b_low):
    def dot(a, b):
        return jnp.dot(a, b, preferred_element_type=jnp.float32)

    return dot(a_high, b_high) + (dot(a_high, b_low) + dot(a_low, b_high))


def spectra_kernel(zsel, half_taps, aliased, *refs):
    x_ref, bh_ref, bl_ref, fh, fl, tc, ts, sh, sl = refs[:9]
    out_ref, done_ref = refs[10:] if aliased else refs[9:]
    done_ref[...] = jnp.zeros_like(done_ref)
    cols = tc.shape[0]
    outs = cols // 2
    x = x_ref[...]
    x = x.reshape(-1, x.shape[-1])
    if x.shape[1] != cols:
        x = jnp.concatenate(
            [x[:, i * cols : (i + 1) * cols] for i in range(x.shape[1] // cols)], axis=0
        )
    x_high, x_low = split(x.T)
    first = dot3(x_high, x_low, fh[...], fl[...])
    re, im = first[:, :RADIX], first[:, RADIX:]
    mid_re = re * tc[...] + im * ts[...]
    mid_im = im * tc[...] - re * ts[...]
    re_high, re_low = split(mid_re)
    im_high, im_low = split(mid_im)

    def block(a, b):
        return jnp.concatenate(
            [jnp.concatenate([a, b], axis=1), jnp.concatenate([b, -a], axis=1)], axis=0
        )

    spec = dot3(sh[...], sl[...], block(re_high, im_high), block(re_low, im_low))
    row = lax.broadcasted_iota(jnp.int32, (outs, RADIX), 0)
    lane = lax.broadcasted_iota(jnp.int32, (outs, RADIX), 1)
    even, odd = [], []
    for part in (spec[:, :RADIX], spec[:, RADIX:]):
        down = jnp.where(row == 0, 0.0, pltpu.roll(part, 1, 0))
        up = jnp.where(row == outs - 1, 0.0, pltpu.roll(part, outs - 1, 0))
        here = jnp.where(lane < half_taps, down, part)
        after = jnp.where(lane < half_taps, part, up)
        even.append(here)
        odd += [here[:, LANES:], after[:, :LANES]]
    window = jnp.concatenate(
        [jnp.concatenate(even, axis=1), jnp.concatenate(odd, axis=1)], axis=0
    )
    w_high, w_low = split(window)
    got = dot3(w_high, w_low, bh_ref[0], bl_ref[0])
    for z in range(zsel):
        at = 2 * z * LANES
        real, imag = got[:, at : at + LANES], got[:, at + LANES : at + 2 * LANES]
        power = real * real + imag * imag
        for e in range(2):
            out_ref[0, pl.ds(e * zsel + z, outs, 2 * zsel), :] = power[e * outs : (e + 1) * outs]


def spectra(x, band_high, band_low, consts, zsel, taps, trials, first_trial, so_far):
    cols = consts[2].shape[0]
    outs = cols // 2
    rows = 2 * outs * zsel
    if x.shape[-1] % cols == 0:
        here = x.shape[1]
        x_spec = pl.BlockSpec((x.shape[0], 1, SUBS, x.shape[-1]), lambda t: (0, t, 0, 0))
    else:
        here = x.shape[1]
        x = x.transpose(1, 0, 2, 3).reshape(here, RADIX, cols)
        x_spec = pl.BlockSpec((1, RADIX, cols), lambda t: (t, 0, 0))
    band_spec = pl.BlockSpec(
        (1,) + band_high.shape[1:], lambda t: (first_trial + t, 0, 0)
    )
    whole = [pl.BlockSpec(c.shape, lambda t: (0, 0)) for c in consts]
    aliased = so_far is not None
    more = [so_far] if aliased else []
    macs = here * (cols * RADIX * 2 * RADIX + outs * 2 * cols * 2 * RADIX + 2 * outs * 4 * RADIX * RADIX)
    return pl.pallas_call(
        functools.partial(spectra_kernel, zsel, taps // 2, aliased),
        grid=(here,),
        out_shape=[
            jax.ShapeDtypeStruct((trials, rows, LANES), jnp.float32),
            jax.ShapeDtypeStruct((SUBS, LANES), jnp.float32),
        ],
        in_specs=[x_spec, band_spec, band_spec, *whole]
        + [pl.BlockSpec(memory_space=pl.ANY)] * len(more),
        out_specs=[
            pl.BlockSpec((1, rows, LANES), lambda t: (first_trial + t, 0, 0)),
            pl.BlockSpec((SUBS, LANES), lambda t: (0, 0)),
        ],
        input_output_aliases={9: 0} if aliased else {},
        compiler_params=pltpu.CompilerParams(vmem_limit_bytes=LIMIT),
        cost_estimate=pl.CostEstimate(
            flops=6 * macs, bytes_accessed=here * 2 * 1024 * 1024, transcendentals=0
        ),
        name="spectra",
    )(x, band_high, band_low, *consts, *more)


def after_kernel(value_ref, done_ref, out_ref):
    del value_ref, done_ref, out_ref


def after(value, done):
    anywhere = pl.BlockSpec(memory_space=pl.ANY)
    return pl.pallas_call(
        after_kernel,
        out_shape=jax.ShapeDtypeStruct(value.shape, value.dtype),
        in_specs=[anywhere, anywhere],
        out_specs=anywhere,
        input_output_aliases={0: 0},
        name="after",
    )(value, done)


def on_device(signal, tree_picks, tree_delays, template_bank, template_pick):
    band_count = lax.axis_size("band")
    time_count = lax.axis_size("tm")
    everyone = band_count * time_count
    sections = LOGCD + band_count.bit_length() - 1
    rim_depth = sections * MAXD
    channels = CH_DEV * band_count
    samples = signal.shape[1] * time_count
    slab = signal.shape[1] // band_count
    width = slab // SUBS
    trials = CH_DEV // time_count
    last = max(1, 3 * trials // 16)
    counts = [count for count in (trials - last, last) if count]
    zsel = template_pick.shape[2]
    taps = template_bank.shape[2]

    band_high, band_low = bands(template_pick[0], template_bank)

    half = (1 << np.arange(sections))[:, None]
    r = np.arange(channels)[None, :]
    base = r - r % (2 * half) + r % half - r % np.minimum(half, CH_DEV)
    low = tree_picks[0] + base.astype(np.int32)
    high = tree_picks[1] + (base + half).astype(np.int32)
    grid = np.arange(channels).reshape(band_count, time_count, trials).transpose(1, 0, 2)
    firsts = [sum(counts[:q]) for q in range(len(counts))]
    order = np.concatenate(
        [grid[:, :, first : first + count].reshape(-1) for first, count in zip(firsts, counts)]
    ).astype(np.int32)
    tables_of = (low, high, tree_delays, jnp.asarray(order))
    sizes = [everyone * count for count in counts]

    folded = signal.reshape(CH_DEV, band_count, SUBS, width)

    def exchanged(value):
        value = lax.all_to_all(value, "band", split_axis=0, concat_axis=0, tiled=True)
        return value.reshape(channels, SUBS, -1)

    def rim_of(x):
        rim = shifted(x[:, 0, :rim_depth], ("tm", "band"), -1)
        rim = jnp.pad(rim, ((0, 0), (0, LANES - rim_depth)))
        return jnp.broadcast_to(rim[:, None, :], (channels, SUBS, LANES))

    if width % (2 * LANES) == 0:
        span = width // 2
        cut = span + LANES
        x_a = exchanged(folded[..., :cut].transpose(1, 0, 2, 3))
        x_b = after(after(folded[..., cut:].transpose(1, 0, 2, 3), x_a), band_low)
        x_b = exchanged(x_b)
        pieces = tree([x_a], [0], None, tables_of, sizes, width, span, 0, [])
        pieces = tree(
            [x_a, x_b], [span, 0], rim_of(x_a), tables_of, sizes, width, span, 1, pieces
        )
    else:
        x = exchanged(folded.transpose(1, 0, 2, 3))
        pieces = tree([x], [0], rim_of(x), tables_of, sizes, width, width, 0, [])

    consts = [jnp.asarray(c) for c in tables(samples, channels, width, taps)]
    out = None
    for first, count, piece in zip(firsts, counts, pieces):
        piece = piece.reshape(everyone, count, SUBS, width)
        if out is not None:
            piece = after(piece, arrived)
        arrived = lax.all_to_all(piece, ("tm", "band"), split_axis=0, concat_axis=0, tiled=True)
        out, _ = spectra(
            arrived, band_high, band_low, consts, zsel, taps, trials, first, out
        )
    out = out.reshape(trials, samples // 2 // LANES, zsel, LANES).transpose(0, 2, 1, 3)
    return out.reshape(1, trials, zsel, samples // 2)


def solution(mesh):
    in_specs = (P(("beams", "band"), "tm"), P(), P(), P(), P(("beams", "band"), "tm", None))
    out_specs = P(("beams", "band"), "tm", None, None)
    return jax.shard_map(
        on_device, mesh=mesh, in_specs=in_specs, out_specs=out_specs, check_vma=False
    )
```
